768 devices in a mesh: dp: 12 (over x, z_hi), wout: 16 (over y, core), win: 4 (over z_lo).
Axes of the slice: x: 4, y: 8, z: 12 (z_hi: 3, z_lo: 4; z = z_hi * 4 + z_lo), core: 2. Of those that a mesh axis runs over, the one named last changes fastest.
Arguments:
- returned: bfloat16 [144, 256, 6144], P('dp', 'wout', 'win'), may hold values from -6 to 6
- lang_rank: int32 [48], replicated, may hold values from 0 to 11, as said below
- weight_down: bfloat16 [24576, 6144], P('wout', 'win'), may hold values from -0.078125 to 0.078125
- pre_act: bfloat16 [12288, 24576], P(('dp', 'win'), 'wout'), may hold values from -6 to 6
Outputs:
- grad_pre: bfloat16 [12288, 24576], P(('dp', 'win'), 'wout')
The draws below stay inside these ranges and needn't reach their ends.
Inputs may be any that keep to these rules, and one draw needn't show every extreme that they name: `lang_rank`: no language rank holds more than one image of one owner (images g with the same g // 4); one language rank holds one image of every owner, so 12 slots are full there; the other ranks hold fewer and their later slots are unused.
All inputs are finite; a program needn't handle non-finite values.
Results may differ from the reference program's by a relative error of at most 0.015.
Values may be sent and summed in bfloat16 or wider, within the bound.
No kernel may reach another device: no remote copies, remote signals or barrier semaphores. Data moves between devices by JAX's collectives and lax.ppermute only.
A program may use at most 32 MiB of HBM per device.

```python
import jax
import jax.numpy as jnp
from jax import lax

D = 6144
FF = 24576
PATCH = 256
IMG_DEV = 4
IMAGES = 48
HOLD = 12
TOKENS = 12288
N_DP = 12
N_WIN = 4


def shuffle_row(row_key, row_values):
    return jax.random.permutation(row_key, row_values)


def other_ranks(row_key):
    return jax.random.permutation(row_key, N_DP - 1)


def draw_lang_rank(key, part):
    key = jax.random.fold_in(key, 7)
    busy_key, other_key, order_key = jax.random.split(key, 3)
    busiest = jax.random.randint(busy_key, (), 0, N_DP).astype(jnp.int32)
    others = jax.vmap(other_ranks)(jax.random.split(other_key, N_DP)).astype(jnp.int32)
    others = jnp.where(others >= busiest, others + 1, others)
    chosen = jnp.concatenate([jnp.full((N_DP, 1), busiest, jnp.int32), others[:, :IMG_DEV - 1]], axis=1)
    shuffled = jax.vmap(shuffle_row)(jax.random.split(order_key, N_DP), chosen)
    return shuffled.reshape(N_DP * IMG_DEV).astype(jnp.int32)


def levels(key, extent, pieces, least, high):
    level = 1.0
    for axis_at, shards_of in pieces:
        heights = jax.random.uniform(jax.random.fold_in(jax.random.fold_in(key, 6), axis_at), (shards_of,), jnp.float32, least / len(pieces), high / len(pieces))
        level = level * jnp.repeat(jnp.exp(heights), extent[axis_at] // shards_of).reshape((-1,) + (1,) * (len(extent) - 1 - axis_at))
    return level


def noise(rng, extent, deviation, most, pieces=(), kind=jnp.bfloat16):
    values = jax.random.normal(rng, extent, jnp.float32) * deviation
    if len(pieces) > 0:
        values = levels(rng, extent, pieces, -0.22, 0.18) * values
    return jnp.clip(values, min=-most, max=most).astype(kind)


def setup_inputs(seed: int = 0) -> dict:
    key_of = jax.random.split(jax.random.key(seed), 5)
    returned = noise(key_of[0], (N_DP * HOLD, PATCH, D), 1.0, 6.0, ((0, 12), (1, 16), (2, 4)))
    lang_rank = draw_lang_rank(jax.random.fold_in(key_of[4], 71), 0)
    weight_down = noise(key_of[2], (FF, D), D ** -0.5, 0.078125, ((0, 16), (1, 4)))
    pre_act = noise(key_of[3], (TOKENS, FF), 1.0, 6.0, ((0, 48), (1, 16)))
    return dict(returned=returned, lang_rank=lang_rank, weight_down=weight_down, pre_act=pre_act)


def gelu_slope(values):
    cdf = 0.5 * (1.0 + lax.erf(values * 0.7071067811865476))
    density = jnp.exp(-0.5 * values * values) * 0.3989422804014327
    return cdf + values * density


def reference(returned, lang_rank, weight_down, pre_act):
    ranks = jnp.arange(HOLD, dtype=jnp.int32)
    onehot = (lang_rank[:, None] == ranks[None, :]).astype(jnp.int32)
    before = jnp.cumsum(onehot, axis=0) - onehot
    position = jnp.sum(before * onehot, axis=1).astype(jnp.int32)
    slot_index = (lang_rank.astype(jnp.int32) * HOLD + position).astype(jnp.int32)
    block_width = D // N_WIN
    pre_images = pre_act.reshape(IMAGES, PATCH, FF)

    def one_image(inputs):
        slot, pre_rows = inputs
        grad_rows = lax.dynamic_index_in_dim(returned, slot, 0, keepdims=False)
        summed = jnp.zeros((PATCH, FF), jnp.float32)
        for block in range(N_WIN):
            left = grad_rows[:, block * block_width:(block + 1) * block_width]
            right = weight_down[:, block * block_width:(block + 1) * block_width]
            partial_value = lax.dot_general(left, right, (((1,), (1,)), ((), ())), preferred_element_type=jnp.float32)
            partial_value = lax.optimization_barrier(partial_value.astype(jnp.bfloat16))
            summed = summed + partial_value.astype(jnp.float32)
        return (summed * gelu_slope(pre_rows.astype(jnp.float32))).astype(jnp.bfloat16)

    result = lax.map(one_image, (slot_index, pre_images))
    return result.reshape(TOKENS, FF)
```

```python
import functools

import jax
import jax.numpy as jnp
from jax import lax
from jax.experimental import pallas as pl
from jax.experimental.pallas import tpu as pltpu
from jax.sharding import PartitionSpec as P

NX, NZH, NY, NW = 4, 3, 8, 4
NZ = NZH * NW
ROWS = 16
OWNERS = NX * NZH
PER_OWNER = 4
HIDDEN_TILE = 512


def gelu_slope(values):
    cdf = 0.5 * (1.0 + lax.erf(values * 0.7071067811865476))
    density = jnp.exp(-0.5 * values * values) * 0.3989422804014327
    return cdf + values * density


def x_perm(step):
    return [(x * NZH + z, (x + step) % NX * NZH + z) for x in range(NX) for z in range(NZH)]


def zh_perm(step):
    return [(x * NZH + z, x * NZH + (z + step) % NZH) for x in range(NX) for z in range(NZH)]


def y_perm(step):
    return [(y * 2 + c, (y + step) % NY * 2 + c) for y in range(NY) for c in range(2)]


def z_perm(step):
    pairs = []
    for x in range(NX):
        for z in range(NZ):
            to = (z + step) % NZ
            pairs.append(((x * NZH + z // NW) * NW + z % NW, (x * NZH + to // NW) * NW + to % NW))
    return pairs


CORE_SWAP = [(w, w ^ 1) for w in range(2 * NY)]


def params():
    return pltpu.CompilerParams(vmem_limit_bytes=40 * 1024 * 1024)


def rank_blocks_kernel(lang_ref, returned_ref, *out_refs):
    here = lax.axis_index("dp")
    x = here // NZH
    count = jnp.int32(0)
    slots = []
    for owner in range(OWNERS):
        slot = jnp.int32(0)
        for k in range(PER_OWNER):
            hit = lang_ref[owner * PER_OWNER + k] == here
            slot = jnp.where(hit, count, slot)
            count = count + hit.astype(jnp.int32)
        slots.append(slot)
    for j in range(NX):
        to = (x + j) % NX
        for h in range(NZH):
            slot = slots[h]
            for other in range(1, NX):
                slot = jnp.where(to == other, slots[other * NZH + h], slot)
            out_refs[j][h] = returned_ref[slot]


def window_positions(z, y):
    far = jnp.where(y < NY // 2, z + 2, z + NZ - 2) % NZ
    return [far, (z + 1) % NZ, (z + NZ - 1) % NZ, z]


def window_blocks_kernel(lang_ref, *refs):
    in_refs, out_refs = refs[:NX], refs[NX:]
    here = lax.axis_index("dp")
    x, zh = here // NZH, here % NZH
    y = lax.axis_index("wout") // 2
    w = lax.axis_index("win")
    for out_ref, step in zip(out_refs, (0, 1, NZH - 1)):
        z = (zh + step) % NZH * NW + w
        for s, position in enumerate(window_positions(z, y)):
            rank = lang_ref[x * NZ + position]
            offset = (x + NX - rank // NZH) % NX
            owner = position // NW
            block = in_refs[0][owner]
            for j in range(1, NX):
                block = jnp.where(offset == j, in_refs[j][owner], block)
            out_ref[s] = block


def window_pick_kernel(lang_ref, own_ref, below_ref, above_ref, out_ref):
    here = lax.axis_index("dp")
    x, zh = here // NZH, here % NZH
    y = lax.axis_index("wout") // 2
    z = zh * NW + lax.axis_index("win")
    for s, position in enumerate(window_positions(z, y)):
        step = (zh + NZH - lang_ref[x * NZ + position] % NZH) % NZH
        block = jnp.where(step == 1, below_ref[s], own_ref[s])
        out_ref[s] = jnp.where(step == 2, above_ref[s], block)


def assemble_kernel(*refs):
    in_refs, (far_ref, near_ref, own_ref) = refs[:NY], refs[NY:]
    y = lax.axis_index("wout") // 2
    for i, ref in enumerate(in_refs):
        back = i if i <= NY // 2 else NY // 2 - i
        at = (y + NY - back) % NY
        far_ref[at] = ref[0]
        near_ref[0, at] = ref[1]
        near_ref[1, at] = ref[2]
        own_ref[at] = ref[3]


def product_kernel(splits, tiles, rows_ref, own_ref, sibling_ref, *out_refs):
    step = pl.program_id(0)

    def run(weight_ref):
        value = lax.dot_general(
            rows_ref[...], weight_ref[...], (((1,), (1,)), ((), ())), preferred_element_type=jnp.float32
        ).astype(jnp.bfloat16)
        start = 0
        for out_ref, size in zip(out_refs, splits):
            out_ref[...] = value[start:start + size]
            start += size

    @pl.when(step < tiles)
    def _():
        run(own_ref)

    @pl.when(step >= tiles)
    def _():
        run(sibling_ref)


def product(rows, own, sibling, splits):
    hidden, width = own.shape
    tiles = hidden // HIDDEN_TILE
    return pl.pallas_call(
        functools.partial(product_kernel, splits, tiles),
        grid=(2 * tiles,),
        in_specs=[
            pl.BlockSpec(rows.shape, lambda i: (0, 0)),
            pl.BlockSpec((HIDDEN_TILE, width), lambda i: (jnp.minimum(i, tiles - 1), 0)),
            pl.BlockSpec((HIDDEN_TILE, width), lambda i: (jnp.maximum(i - tiles, 0), 0)),
        ],
        out_specs=[pl.BlockSpec((size, HIDDEN_TILE), lambda i: (0, i)) for size in splits],
        out_shape=[jax.ShapeDtypeStruct((size, 2 * hidden), jnp.bfloat16) for size in splits],
        compiler_params=params(),
    )(rows, own, sibling)


def local(returned, lang_rank, weight_down, pre_act):
    core = lax.axis_index("wout") % 2
    width = returned.shape[2]
    hidden = weight_down.shape[0]
    smem = pl.BlockSpec(memory_space=pltpu.SMEM)
    vmem = pl.BlockSpec(memory_space=pltpu.VMEM)

    sibling = lax.ppermute(weight_down, "wout", CORE_SWAP)
    pre_split = pre_act.reshape(NY, 2, ROWS, hidden)
    pre_own = lax.dynamic_index_in_dim(pre_split, core, 1, keepdims=False)
    pre_sent = lax.dynamic_index_in_dim(pre_split, 1 - core, 1, keepdims=False)
    pre_sibling = lax.ppermute(pre_sent, "wout", CORE_SWAP)

    held = pl.pallas_call(
        rank_blocks_kernel,
        in_specs=[smem, vmem],
        out_specs=[vmem] * NX,
        out_shape=[jax.ShapeDtypeStruct((NZH, ROWS, width), jnp.bfloat16)] * NX,
        compiler_params=params(),
    )(lang_rank, returned)
    columns = [held[0]] + [lax.ppermute(held[j], "dp", x_perm(j)) for j in range(1, NX)]

    block4 = jax.ShapeDtypeStruct((4, ROWS, width), jnp.bfloat16)
    window_own, window_up, window_down = pl.pallas_call(
        window_blocks_kernel,
        in_specs=[smem] + [vmem] * NX,
        out_specs=[vmem] * 3,
        out_shape=[block4] * 3,
        compiler_params=params(),
    )(lang_rank, *columns)
    from_below = lax.ppermute(window_up, "dp", zh_perm(1))
    from_above = lax.ppermute(window_down, "dp", zh_perm(-1))
    window = pl.pallas_call(
        window_pick_kernel,
        in_specs=[smem] + [vmem] * 3,
        out_specs=vmem,
        out_shape=block4,
        compiler_params=params(),
    )(lang_rank, window_own, from_below, from_above)

    up, down = [window], [window]
    for step in range(4):
        up.append(lax.ppermute(up[-1], "wout", y_perm(1)))
        if step < 3:
            down.append(lax.ppermute(down[-1], "wout", y_perm(-1)))
    far, near, own = pl.pallas_call(
        assemble_kernel,
        in_specs=[vmem] * NY,
        out_specs=[vmem] * 3,
        out_shape=[
            jax.ShapeDtypeStruct((NY, ROWS, width), jnp.bfloat16),
            jax.ShapeDtypeStruct((2, NY, ROWS, width), jnp.bfloat16),
            jax.ShapeDtypeStruct((NY, ROWS, width), jnp.bfloat16),
        ],
        compiler_params=params(),
    )(*up, *down[1:])
    rows = NY * ROWS
    half = rows // 2
    far_up, far_down = product(far.reshape(rows, width), weight_down, sibling, (half, half))
    up_add, up_plain, down_plain, down_add = product(
        near.reshape(2 * rows, width), weight_down, sibling, (half,) * 4
    )
    (mine,) = product(own.reshape(rows, width), weight_down, sibling, (rows,))

    ring = ("dp", "win")
    add_up = lax.ppermute(far_up, ring, z_perm(1))
    add_down = lax.ppermute(far_down, ring, z_perm(-1))
    got_up_plain = lax.ppermute(up_plain, ring, z_perm(1))
    got_down_plain = lax.ppermute(down_plain, ring, z_perm(-1))

    def add(a, b):
        return (a.astype(jnp.float32) + b.astype(jnp.float32)).astype(jnp.bfloat16)

    got_up = lax.ppermute(add(up_add, add_up), ring, z_perm(1))
    got_down = lax.ppermute(add(down_add, add_down), ring, z_perm(-1))

    def finish(part, got_a, got_b, pre_a, pre_b):
        total = part.astype(jnp.float32) + got_a.astype(jnp.float32) + got_b.astype(jnp.float32)
        return [
            (total[:, i * hidden:(i + 1) * hidden] * gelu_slope(pre.reshape(half, hidden).astype(jnp.float32))).astype(jnp.bfloat16)
            for i, pre in enumerate((pre_a, pre_b))
        ]

    first = finish(mine[:half], got_up, got_down_plain, pre_own[:NY // 2], pre_sibling[:NY // 2])
    second = finish(mine[half:], got_up_plain, got_down, pre_own[NY // 2:], pre_sibling[NY // 2:])
    kept = jnp.concatenate([first[0], second[0]], axis=0)
    sent = jnp.concatenate([first[1], second[1]], axis=0)
    other = lax.ppermute(sent, "wout", CORE_SWAP)
    kept, other = (v.reshape(NY, 1, ROWS, hidden) for v in (kept, other))
    even = jnp.where(core == 0, kept, other)
    odd = jnp.where(core == 0, other, kept)
    return jnp.concatenate([even, odd], axis=1).reshape(2 * rows, hidden)


def solution(mesh):
    in_specs = (P("dp", "wout", "win"), P(), P("wout", "win"), P(("dp", "win"), "wout"))
    out_specs = P(("dp", "win"), "wout")
    return jax.shard_map(local, mesh=mesh, in_specs=in_specs, out_specs=out_specs, check_vma=False)
```

```python
import functools

import jax
import jax.numpy as jnp
from jax import lax
from jax.experimental import pallas as pl
from jax.experimental.pallas import tpu as pltpu
from jax.sharding import PartitionSpec as P

NX, NZH, NY, NW = 4, 3, 8, 4
NZ = NZH * NW
ROWS = 16
OWNERS = NX * NZH
PER_OWNER = 4
SLOTS = 4
HALF = NY // 2
HIDDEN_TILE = 768

X_GROUPS = [[x * NZH + z for x in range(NX)] for z in range(NZH)]
PARITY_GROUPS = [[y * 2 + c for y in range(p, NY, 2)] for p in range(2) for c in range(2)]
CORE_SWAP = [(w, w ^ 1) for w in range(2 * NY)]
RING = ("dp", "wout", "win")


def gelu_slope(values):
    cdf = 0.5 * (1.0 + lax.erf(values * 0.7071067811865476))
    density = jnp.exp(-0.5 * values * values) * 0.3989422804014327
    return cdf + values * density


def ring_perm(step):
    def index(x, z, w):
        return ((x * NZH + z // NW) * 2 * NY + w) * NW + z % NW

    return [
        (index(x, z, w), index(x, (z + (step if w % 2 == 0 else -step)) % NZ, w))
        for x in range(NX) for z in range(NZ) for w in range(2 * NY)
    ]


def zh_perm(step):
    return [(x * NZH + z, x * NZH + (z + step) % NZH) for x in range(NX) for z in range(NZH)]


def y_perm(step):
    return [(y * 2 + c, (y + step) % NY * 2 + c) for y in range(NY) for c in range(2)]


def params():
    return pltpu.CompilerParams(vmem_limit_bytes=40 * 1024 * 1024)


def rank_blocks_kernel(lang_ref, returned_ref, out_ref):
    here = lax.axis_index("dp")
    count = jnp.int32(0)
    for owner in range(OWNERS):
        slot = jnp.int32(0)
        for k in range(PER_OWNER):
            hit = lang_ref[owner * PER_OWNER + k] == here
            slot = jnp.where(hit, count, slot)
            count = count + hit.astype(jnp.int32)
        out_ref[owner // NZH, owner % NZH * ROWS:(owner % NZH + 1) * ROWS] = returned_ref[slot]


def window_positions(z, core):
    sign = 1 - 2 * core
    return [(z + NZ + sign * step) % NZ for step in (2, 1, -1, 0)]


def window_blocks_kernel(lang_ref, in_ref, *out_refs):
    here = lax.axis_index("dp")
    column = here // NZH
    core = lax.axis_index("wout") % 2
    w = lax.axis_index("win")
    for h in range(NZH):
        for s, position in enumerate(window_positions((here + h) % NZH * NW + w, core)):
            rank = lang_ref[column * NZ + position]
            start = pl.multiple_of(position // NW * ROWS, ROWS)
            out_refs[h][s * ROWS:(s + 1) * ROWS] = in_ref[rank // NZH, pl.ds(start, ROWS)]


def window_pick_kernel(lang_ref, *refs):
    in_refs, out_ref = refs[:NZH], refs[NZH]
    here = lax.axis_index("dp")
    core = lax.axis_index("wout") % 2
    z = here % NZH * NW + lax.axis_index("win")
    for s, position in enumerate(window_positions(z, core)):
        rows = slice(s * ROWS, (s + 1) * ROWS)
        back = (here + NZH - lang_ref[here // NZH * NZ + position] % NZH) % NZH
        block = in_refs[0][rows]
        for j in range(1, NZH):
            block = jnp.where(back == j, in_refs[j][rows], block)
        out_ref[rows] = block


def product_kernel(count, *refs):
    rows_refs, (sibling_ref, own_hbm), out_refs = refs[:count], refs[count:count + 2], refs[count + 2:-2]
    own_ref, sem = refs[-2:]
    copy = pltpu.make_async_copy(own_hbm, own_ref, sem)
    copy.start()
    hidden, width = sibling_ref.shape
    rows = jnp.concatenate(
        [
            ref[:, s * ROWS:(s + 1) * ROWS].reshape(-1, width)
            for s in range(SLOTS) for ref in rows_refs
        ],
        axis=0,
    )

    def run(weight_ref, start):
        for tile in range(0, hidden, HIDDEN_TILE):
            value = lax.dot_general(
                rows, weight_ref[tile:tile + HIDDEN_TILE], (((1,), (1,)), ((), ())),
                preferred_element_type=jnp.float32,
            ).astype(jnp.bfloat16)
            for s, out_ref in enumerate(out_refs):
                size = out_ref.shape[0]
                out_ref[:, start + tile:start + tile + HIDDEN_TILE] = value[s * size:(s + 1) * size]

    run(sibling_ref, hidden)
    copy.wait()
    run(own_ref, 0)


def product(blocks, own, sibling):
    hidden, width = own.shape
    vmem = pl.BlockSpec(memory_space=pltpu.VMEM)
    return pl.pallas_call(
        functools.partial(product_kernel, len(blocks)),
        in_specs=[vmem] * (len(blocks) + 1) + [pl.BlockSpec(memory_space=pl.ANY)],
        out_specs=[vmem] * SLOTS,
        out_shape=[jax.ShapeDtypeStruct((HALF * ROWS, 2 * hidden), jnp.bfloat16)] * SLOTS,
        scratch_shapes=[pltpu.VMEM((hidden, width), jnp.bfloat16), pltpu.SemaphoreType.DMA],
        compiler_params=params(),
    )(*blocks, sibling, own)


def parity_and_core():
    place = lax.axis_index("wout")
    return place // 2 % 2, place % 2


def split_kernel(pre_ref, kept_ref, sent_ref):
    parity, core = parity_and_core()
    for h in range(2):
        for j in range(HALF):
            kept_ref[h, j] = pre_ref[j, (parity + h) % 2, core]
            sent_ref[h, j] = pre_ref[j, (parity + h) % 2, 1 - core]


def finish_kernel(*refs):
    parts, (pre_own, pre_sibling, kept_ref, sent_ref) = refs[:6], refs[6:]
    hidden = pre_own.shape[3]
    for h in range(2):
        mine, ahead, behind = parts[3 * h:3 * h + 3]
        for i, (pre_ref, out_ref) in enumerate(((pre_own, kept_ref), (pre_sibling, sent_ref))):
            for j in range(HALF):
                at = slice(j * ROWS, (j + 1) * ROWS), slice(i * hidden, (i + 1) * hidden)
                total = mine[at].astype(jnp.float32) + ahead[at].astype(jnp.float32) + behind[at].astype(jnp.float32)
                out_ref[h, j] = (total * gelu_slope(pre_ref[h, j].astype(jnp.float32))).astype(jnp.bfloat16)


def join_kernel(kept_ref, other_ref, out_ref):
    parity, core = parity_and_core()
    for h in range(2):
        for j in range(HALF):
            out_ref[j, (parity + h) % 2, core] = kept_ref[h, j]
            out_ref[j, (parity + h) % 2, 1 - core] = other_ref[h, j]


def local(returned, lang_rank, weight_down, pre_act):
    width = returned.shape[2]
    hidden = weight_down.shape[0]
    smem = pl.BlockSpec(memory_space=pltpu.SMEM)
    vmem = pl.BlockSpec(memory_space=pltpu.VMEM)

    def move(kernel, out, *values, count=None):
        shape = jax.ShapeDtypeStruct(out + (width,), jnp.bfloat16)
        return pl.pallas_call(
            kernel,
            in_specs=[smem] + [vmem] * len(values),
            out_specs=vmem if count is None else [vmem] * count,
            out_shape=shape if count is None else [shape] * count,
            compiler_params=params(),
        )(lang_rank, *values)

    held = move(rank_blocks_kernel, (NX, NZH * ROWS), returned)
    held = lax.all_to_all(held, "dp", 0, 0, axis_index_groups=X_GROUPS)
    windows = move(window_blocks_kernel, (SLOTS * ROWS,), held, count=NZH)
    weight_down, pre_act, _ = lax.optimization_barrier((weight_down, pre_act, windows[1]))
    sibling = lax.ppermute(weight_down, "wout", CORE_SWAP)
    halves = jax.ShapeDtypeStruct((2, HALF, ROWS, hidden), jnp.bfloat16)
    pre_own, pre_sent = pl.pallas_call(
        split_kernel,
        in_specs=[vmem],
        out_specs=[vmem] * 2,
        out_shape=[halves] * 2,
        compiler_params=params(),
    )(pre_act.reshape(HALF, 2, 2, ROWS, hidden))
    pre_sibling = lax.ppermute(pre_sent, "wout", CORE_SWAP)
    windows = [windows[0]] + [lax.ppermute(windows[j], "dp", zh_perm(j)) for j in range(1, NZH)]
    window = move(window_pick_kernel, (SLOTS * ROWS,), *windows)
    near = lax.all_gather(window, "wout", axis_index_groups=PARITY_GROUPS)
    others = [
        lax.ppermute(near[:HALF // 2], "wout", y_perm(1)),
        lax.ppermute(near[HALF // 2:], "wout", y_perm(-1)),
    ]

    parts = []
    for blocks in ([near], others):
        far, ahead, behind, mine = product(blocks, weight_down, sibling)
        far = lax.ppermute(far, RING, ring_perm(1))
        behind = lax.ppermute(behind, RING, ring_perm(-1))
        ahead = (ahead.astype(jnp.float32) + far.astype(jnp.float32)).astype(jnp.bfloat16)
        parts += [mine, lax.ppermute(ahead, RING, ring_perm(1)), behind]

    kept, sent = pl.pallas_call(
        finish_kernel,
        in_specs=[vmem] * 8,
        out_specs=[vmem] * 2,
        out_shape=[halves] * 2,
        compiler_params=params(),
    )(*parts, pre_own, pre_sibling)
    other = lax.ppermute(sent, "wout", CORE_SWAP)
    out = pl.pallas_call(
        join_kernel,
        in_specs=[vmem] * 2,
        out_specs=vmem,
        out_shape=jax.ShapeDtypeStruct((HALF, 2, 2, ROWS, hidden), jnp.bfloat16),
        compiler_params=params(),
    )(kept, other)
    return out.reshape(2 * NY * ROWS, hidden)


def solution(mesh):
    in_specs = (P("dp", "wout", "win"), P(), P("wout", "win"), P(("dp", "win"), "wout"))
    out_specs = P(("dp", "win"), "wout")
    return jax.shard_map(local, mesh=mesh, in_specs=in_specs, out_specs=out_specs, check_vma=False)
```

```python
import jax
import jax.numpy as jnp
from jax import lax
from jax.experimental import pallas as pl
from jax.experimental.pallas import tpu as pltpu
from jax.sharding import PartitionSpec as P

NX, NZH, NY, NW = 4, 3, 8, 4
NZ = NZH * NW
ROWS = 16
OWNERS = NX * NZH
PER_OWNER = 4
SLOTS = 4
HALF = NY // 2
HIDDEN_TILE = 768

X_GROUPS = [[x * NZH + z for x in range(NX)] for z in range(NZH)]
PARITY_GROUPS = [[y * 2 + c for y in range(p, NY, 2)] for p in range(2) for c in range(2)]
CORE_SWAP = [(w, w ^ 1) for w in range(2 * NY)]
PAIR_SWAP = [(w, w ^ 2) for w in range(2 * NY)]
RING = ("dp", "wout", "win")


def gelu_slope(values):
    cdf = 0.5 * (1.0 + lax.erf(values * 0.7071067811865476))
    density = jnp.exp(-0.5 * values * values) * 0.3989422804014327
    return cdf + values * density


def ring_perm(step):
    def index(x, z, w):
        return ((x * NZH + z // NW) * 2 * NY + w) * NW + z % NW

    return [
        (index(x, z, w), index(x, (z + (step if w % 2 == 0 else -step)) % NZ, w))
        for x in range(NX) for z in range(NZ) for w in range(2 * NY)
    ]


def zh_perm(step):
    return [(x * NZH + z, x * NZH + (z + step) % NZH) for x in range(NX) for z in range(NZH)]


def params():
    return pltpu.CompilerParams(vmem_limit_bytes=40 * 1024 * 1024)


def rank_blocks_kernel(lang_ref, returned_ref, out_ref):
    here = lax.axis_index("dp")
    count = jnp.int32(0)
    for owner in range(OWNERS):
        slot = jnp.int32(0)
        for k in range(PER_OWNER):
            hit = lang_ref[owner * PER_OWNER + k] == here
            slot = jnp.where(hit, count, slot)
            count = count + hit.astype(jnp.int32)
        out_ref[owner // NZH, owner % NZH * ROWS:(owner % NZH + 1) * ROWS] = returned_ref[slot]


def window_positions(z, core):
    sign = 1 - 2 * core
    return [(z + NZ + sign * step) % NZ for step in (2, 1, -1, 0)]


def window_blocks_kernel(lang_ref, in_ref, *out_refs):
    here = lax.axis_index("dp")
    column = here // NZH
    core = lax.axis_index("wout") % 2
    w = lax.axis_index("win")
    for h in range(NZH):
        for s, position in enumerate(window_positions((here + h) % NZH * NW + w, core)):
            rank = lang_ref[column * NZ + position]
            start = pl.multiple_of(position // NW * ROWS, ROWS)
            out_refs[h][s * ROWS:(s + 1) * ROWS] = in_ref[rank // NZH, pl.ds(start, ROWS)]


def window_pick_kernel(lang_ref, *refs):
    in_refs, out_ref = refs[:NZH], refs[NZH]
    here = lax.axis_index("dp")
    core = lax.axis_index("wout") % 2
    z = here % NZH * NW + lax.axis_index("win")
    for s, position in enumerate(window_positions(z, core)):
        rows = slice(s * ROWS, (s + 1) * ROWS)
        back = (here + NZH - lang_ref[here // NZH * NZ + position] % NZH) % NZH
        block = in_refs[0][rows]
        for j in range(1, NZH):
            block = jnp.where(back == j, in_refs[j][rows], block)
        out_ref[rows] = block


def product_kernel(rows_ref, sibling_ref, own_hbm, *refs):
    out_refs, (own_ref, sem) = refs[:-2], refs[-2:]
    copy = pltpu.make_async_copy(own_hbm, own_ref, sem)
    copy.start()
    hidden, width = sibling_ref.shape
    rows = jnp.concatenate(
        [rows_ref[:, s * ROWS:(s + 1) * ROWS].reshape(-1, width) for s in range(SLOTS)], axis=0
    )

    def run(weight_ref, start):
        for tile in range(0, hidden, HIDDEN_TILE):
            value = lax.dot_general(
                rows, weight_ref[tile:tile + HIDDEN_TILE], (((1,), (1,)), ((), ())),
                preferred_element_type=jnp.float32,
            ).astype(jnp.bfloat16)
            for s, out_ref in enumerate(out_refs):
                size = out_ref.shape[0]
                out_ref[:, start + tile:start + tile + HIDDEN_TILE] = value[s * size:(s + 1) * size]

    run(sibling_ref, hidden)
    copy.wait()
    run(own_ref, 0)


def product(blocks, own, sibling):
    hidden, width = own.shape
    vmem = pl.BlockSpec(memory_space=pltpu.VMEM)
    return pl.pallas_call(
        product_kernel,
        in_specs=[vmem] * 2 + [pl.BlockSpec(memory_space=pl.ANY)],
        out_specs=[vmem] * SLOTS,
        out_shape=[jax.ShapeDtypeStruct((HALF * ROWS, 2 * hidden), jnp.bfloat16)] * SLOTS,
        scratch_shapes=[pltpu.VMEM((hidden, width), jnp.bfloat16), pltpu.SemaphoreType.DMA],
        compiler_params=params(),
    )(blocks, sibling, own)


def parity_and_core():
    place = lax.axis_index("wout")
    return place // 2 % 2, place % 2


def half_sums(parts, j, i, hidden):
    total = 0.0
    for ref in parts:
        total = total + ref[j * ROWS:(j + 1) * ROWS, i * hidden:(i + 1) * hidden].astype(jnp.float32)
    return total


def send_kernel(*refs):
    parts, sent_ref = (refs[:3], refs[3:6]), refs[6]
    for h in range(2):
        for j in range(HALF):
            sent_ref[h, j] = half_sums(parts[h], j, 1, sent_ref.shape[3]).astype(jnp.bfloat16)


def keep_kernel(*refs):
    parts, (pre_ref, kept_ref, slope_ref) = (refs[:3], refs[3:6]), refs[6:]
    parity, core = parity_and_core()
    for h in range(2):
        for j in range(HALF):
            slope = gelu_slope(pre_ref[j, (parity + h) % 2, core].astype(jnp.float32))
            kept_ref[h, j] = (half_sums(parts[h], j, 0, kept_ref.shape[3]) * slope).astype(jnp.bfloat16)
            slope_ref[h, j] = gelu_slope(pre_ref[j, (parity + h) % 2, 1 - core].astype(jnp.float32))


def join_kernel(kept_ref, slope_ref, other_ref, out_ref):
    parity, core = parity_and_core()
    for h in range(2):
        for j in range(HALF):
            out_ref[j, (parity + h) % 2, core] = kept_ref[h, j]
            other = other_ref[h, j].astype(jnp.float32) * slope_ref[h, j]
            out_ref[j, (parity + h) % 2, 1 - core] = other.astype(jnp.bfloat16)


def local(returned, lang_rank, weight_down, pre_act):
    width = returned.shape[2]
    hidden = weight_down.shape[0]
    smem = pl.BlockSpec(memory_space=pltpu.SMEM)
    vmem = pl.BlockSpec(memory_space=pltpu.VMEM)

    def move(kernel, out, *values, count=None):
        shape = jax.ShapeDtypeStruct(out + (width,), jnp.bfloat16)
        return pl.pallas_call(
            kernel,
            in_specs=[smem] + [vmem] * len(values),
            out_specs=vmem if count is None else [vmem] * count,
            out_shape=shape if count is None else [shape] * count,
            compiler_params=params(),
        )(lang_rank, *values)

    held = move(rank_blocks_kernel, (NX, NZH * ROWS), returned)
    held = lax.all_to_all(held, "dp", 0, 0, axis_index_groups=X_GROUPS)
    windows = move(window_blocks_kernel, (SLOTS * ROWS,), held, count=NZH)
    weight_sent, _ = lax.optimization_barrier((weight_down, windows[1]))
    sibling = lax.ppermute(weight_sent, "wout", CORE_SWAP)
    windows = [windows[0]] + [lax.ppermute(windows[j], "dp", zh_perm(j)) for j in range(1, NZH)]
    window = move(window_pick_kernel, (SLOTS * ROWS,), *windows)
    near = lax.all_gather(window, "wout", axis_index_groups=PARITY_GROUPS)
    others = lax.ppermute(near, "wout", PAIR_SWAP)

    parts = []
    for blocks in (near, others):
        far, ahead, behind, mine = product(blocks, weight_down, sibling)
        far = lax.ppermute(far, RING, ring_perm(1))
        behind = lax.ppermute(behind, RING, ring_perm(-1))
        ahead = (ahead.astype(jnp.float32) + far.astype(jnp.float32)).astype(jnp.bfloat16)
        parts += [mine, lax.ppermute(ahead, RING, ring_perm(1)), behind]

    def call(kernel, shapes, *values):
        return pl.pallas_call(
            kernel,
            in_specs=[vmem] * len(values),
            out_specs=[vmem] * len(shapes),
            out_shape=[jax.ShapeDtypeStruct(*shape) for shape in shapes],
            compiler_params=params(),
        )(*values)

    halves = (2, HALF, ROWS, hidden)
    split = (HALF, 2, 2, ROWS, hidden)
    (sent,) = call(send_kernel, [(halves, jnp.bfloat16)], *parts)
    other = lax.ppermute(sent, "wout", CORE_SWAP)
    kept, slope = call(
        keep_kernel,
        [(halves, jnp.bfloat16), (halves, jnp.float32)],
        *parts, pre_act.reshape(split),
    )
    (out,) = call(join_kernel, [(split, jnp.bfloat16)], kept, slope, other)
    return out.reshape(2 * NY * ROWS, hidden)


def solution(mesh):
    in_specs = (P("dp", "wout", "win"), P(), P("wout", "win"), P(("dp", "win"), "wout"))
    out_specs = P(("dp", "win"), "wout")
    return jax.shard_map(local, mesh=mesh, in_specs=in_specs, out_specs=out_specs, check_vma=False)
```

```python
import jax
import jax.numpy as jnp
from jax import lax
from jax.experimental import pallas as pl
from jax.experimental.pallas import tpu as pltpu
from jax.sharding import PartitionSpec as P

NX, NZH, NY, NW = 4, 3, 8, 4
NZ = NZH * NW
ROWS = 16
OWNERS = NX * NZH
PER_OWNER = 4
SLOTS = 4
HALF = NY // 2
HIDDEN_TILE = 768

X_GROUPS = [[x * NZH + z for x in range(NX)] for z in range(NZH)]
PARITY_GROUPS = [[y * 2 + c for y in range(p, NY, 2)] for p in range(2) for c in range(2)]
CORE_SWAP = [(w, w ^ 1) for w in range(2 * NY)]
PAIR_SWAP = [(w, w ^ 2) for w in range(2 * NY)]
RING = ("dp", "wout", "win")


def gelu_slope(values):
    cdf = 0.5 * (1.0 + lax.erf(values * 0.7071067811865476))
    density = jnp.exp(-0.5 * values * values) * 0.3989422804014327
    return cdf + values * density


def ring_perm(step):
    def index(x, z, w):
        return ((x * NZH + z // NW) * 2 * NY + w) * NW + z % NW

    return [
        (index(x, z, w), index(x, (z + (step if w % 2 == 0 else -step)) % NZ, w))
        for x in range(NX) for z in range(NZ) for w in range(2 * NY)
    ]


def zh_perm(step):
    return [(x * NZH + z, x * NZH + (z + step) % NZH) for x in range(NX) for z in range(NZH)]


def params():
    return pltpu.CompilerParams(vmem_limit_bytes=40 * 1024 * 1024)


def rank_blocks_kernel(lang_ref, returned_ref, out_ref):
    here = lax.axis_index("dp")
    count = jnp.int32(0)
    for owner in range(OWNERS):
        slot = jnp.int32(0)
        for k in range(PER_OWNER):
            hit = lang_ref[owner * PER_OWNER + k] == here
            slot = jnp.where(hit, count, slot)
            count = count + hit.astype(jnp.int32)
        out_ref[owner // NZH, owner % NZH * ROWS:(owner % NZH + 1) * ROWS] = returned_ref[slot]


def window_positions(z, core):
    sign = 1 - 2 * core
    return [(z + NZ + sign * step) % NZ for step in (2, 1, -1, 0)]


def window_blocks_kernel(lang_ref, in_ref, *out_refs):
    here = lax.axis_index("dp")
    column = here // NZH
    core = lax.axis_index("wout") % 2
    w = lax.axis_index("win")
    for h in range(NZH):
        for s, position in enumerate(window_positions((here + h) % NZH * NW + w, core)):
            rank = lang_ref[column * NZ + position]
            start = pl.multiple_of(position // NW * ROWS, ROWS)
            out_refs[h][s * ROWS:(s + 1) * ROWS] = in_ref[rank // NZH, pl.ds(start, ROWS)]


def window_pick_kernel(lang_ref, *refs):
    in_refs, out_ref = refs[:NZH], refs[NZH]
    here = lax.axis_index("dp")
    core = lax.axis_index("wout") % 2
    z = here % NZH * NW + lax.axis_index("win")
    for s, position in enumerate(window_positions(z, core)):
        rows = slice(s * ROWS, (s + 1) * ROWS)
        back = (here + NZH - lang_ref[here // NZH * NZ + position] % NZH) % NZH
        block = in_refs[0][rows]
        for j in range(1, NZH):
            block = jnp.where(back == j, in_refs[j][rows], block)
        out_ref[rows] = block


def product_kernel(rows_ref, sibling_ref, own_ref, *out_refs):
    hidden, width = sibling_ref.shape
    rows = jnp.concatenate(
        [rows_ref[:, s * ROWS:(s + 1) * ROWS].reshape(-1, width) for s in range(SLOTS)], axis=0
    )

    def run(weight_ref, start):
        for tile in range(0, hidden, HIDDEN_TILE):
            value = lax.dot_general(
                rows, weight_ref[tile:tile + HIDDEN_TILE], (((1,), (1,)), ((), ())),
                preferred_element_type=jnp.float32,
            ).astype(jnp.bfloat16)
            for s, out_ref in enumerate(out_refs):
                size = out_ref.shape[0]
                out_ref[:, start + tile:start + tile + HIDDEN_TILE] = value[s * size:(s + 1) * size]

    run(sibling_ref, hidden)
    run(own_ref, 0)


def product(blocks, own, sibling):
    hidden, width = own.shape
    vmem = pl.BlockSpec(memory_space=pltpu.VMEM)
    return pl.pallas_call(
        product_kernel,
        in_specs=[vmem] * 3,
        out_specs=[vmem] * SLOTS,
        out_shape=[jax.ShapeDtypeStruct((HALF * ROWS, 2 * hidden), jnp.bfloat16)] * SLOTS,
        compiler_params=params(),
    )(blocks, sibling, own)


def parity_and_core():
    place = lax.axis_index("wout")
    return place // 2 % 2, place % 2


def half_sums(parts, j, i, hidden):
    total = 0.0
    for ref in parts:
        total = total + ref[j * ROWS:(j + 1) * ROWS, i * hidden:(i + 1) * hidden].astype(jnp.float32)
    return total


def send_kernel(*refs):
    parts, sent_ref = (refs[:3], refs[3:6]), refs[6]
    for h in range(2):
        for j in range(HALF):
            sent_ref[h, j] = half_sums(parts[h], j, 1, sent_ref.shape[3]).astype(jnp.bfloat16)


def keep_kernel(*refs):
    parts, (pre_ref, kept_ref, slope_ref) = (refs[:3], refs[3:6]), refs[6:]
    parity, core = parity_and_core()
    for h in range(2):
        for j in range(HALF):
            slope = gelu_slope(pre_ref[j, (parity + h) % 2, core].astype(jnp.float32))
            kept_ref[h, j] = (half_sums(parts[h], j, 0, kept_ref.shape[3]) * slope).astype(jnp.bfloat16)
            slope_ref[h, j] = gelu_slope(pre_ref[j, (parity + h) % 2, 1 - core].astype(jnp.float32))


def join_kernel(kept_ref, slope_ref, other_ref, out_ref):
    parity, core = parity_and_core()
    for h in range(2):
        for j in range(HALF):
            out_ref[j, (parity + h) % 2, core] = kept_ref[h, j]
            other = other_ref[h, j].astype(jnp.float32) * slope_ref[h, j]
            out_ref[j, (parity + h) % 2, 1 - core] = other.astype(jnp.bfloat16)


def local(returned, lang_rank, weight_down, pre_act):
    width = returned.shape[2]
    hidden = weight_down.shape[0]
    smem = pl.BlockSpec(memory_space=pltpu.SMEM)
    vmem = pl.BlockSpec(memory_space=pltpu.VMEM)

    def move(kernel, out, *values, count=None):
        shape = jax.ShapeDtypeStruct(out + (width,), jnp.bfloat16)
        return pl.pallas_call(
            kernel,
            in_specs=[smem] + [vmem] * len(values),
            out_specs=vmem if count is None else [vmem] * count,
            out_shape=shape if count is None else [shape] * count,
            compiler_params=params(),
        )(lang_rank, *values)

    sibling = lax.ppermute(weight_down, "wout", CORE_SWAP)
    held = move(rank_blocks_kernel, (NX, NZH * ROWS), returned)
    held = lax.all_to_all(held, "dp", 0, 0, axis_index_groups=X_GROUPS)
    windows = move(window_blocks_kernel, (SLOTS * ROWS,), held, count=NZH)
    windows = [windows[0]] + [lax.ppermute(windows[j], "dp", zh_perm(j)) for j in range(1, NZH)]
    window = move(window_pick_kernel, (SLOTS * ROWS,), *windows)
    near = lax.all_gather(window, "wout", axis_index_groups=PARITY_GROUPS)
    others = lax.ppermute(near, "wout", PAIR_SWAP)

    parts = []
    for blocks in (near, others):
        far, ahead, behind, mine = product(blocks, weight_down, sibling)
        far = lax.ppermute(far, RING, ring_perm(1))
        behind = lax.ppermute(behind, RING, ring_perm(-1))
        ahead = (ahead.astype(jnp.float32) + far.astype(jnp.float32)).astype(jnp.bfloat16)
        parts += [mine, lax.ppermute(ahead, RING, ring_perm(1)), behind]

    def call(kernel, shapes, *values):
        return pl.pallas_call(
            kernel,
            in_specs=[vmem] * len(values),
            out_specs=[vmem] * len(shapes),
            out_shape=[jax.ShapeDtypeStruct(*shape) for shape in shapes],
            compiler_params=params(),
        )(*values)

    halves = (2, HALF, ROWS, hidden)
    split = (HALF, 2, 2, ROWS, hidden)
    (sent,) = call(send_kernel, [(halves, jnp.bfloat16)], *parts)
    other = lax.ppermute(sent, "wout", CORE_SWAP)
    kept, slope = call(
        keep_kernel,
        [(halves, jnp.bfloat16), (halves, jnp.float32)],
        *parts, pre_act.reshape(split),
    )
    (out,) = call(join_kernel, [(split, jnp.bfloat16)], kept, slope, other)
    return out.reshape(2 * NY * ROWS, hidden)


def solution(mesh):
    in_specs = (P("dp", "wout", "win"), P(), P("wout", "win"), P(("dp", "win"), "wout"))
    out_specs = P(("dp", "win"), "wout")
    return jax.shard_map(local, mesh=mesh, in_specs=in_specs, out_specs=out_specs, check_vma=False)
```

```python
import functools

import jax
import jax.numpy as jnp
from jax import lax
from jax.experimental import pallas as pl
from jax.experimental.pallas import tpu as pltpu
from jax.sharding import PartitionSpec as P

NX, NZH, NY, NW = 4, 3, 8, 4
NZ = NZH * NW
ROWS = 16
OWNERS = NX * NZH
PER_OWNER = 4
SLOTS = 4
HALF = NY // 2
HIDDEN_TILE = 768

X_GROUPS = [[x * NZH + z for x in range(NX)] for z in range(NZH)]
PARITY_GROUPS = [[y * 2 + c for y in range(p, NY, 2)] for p in range(2) for c in range(2)]
CORE_SWAP = [(w, w ^ 1) for w in range(2 * NY)]
RING = ("dp", "wout", "win")


def gelu_slope(values):
    cdf = 0.5 * (1.0 + lax.erf(values * 0.7071067811865476))
    density = jnp.exp(-0.5 * values * values) * 0.3989422804014327
    return cdf + values * density


def ring_perm(step):
    def index(x, z, w):
        return ((x * NZH + z // NW) * 2 * NY + w) * NW + z % NW

    return [
        (index(x, z, w), index(x, (z + (step if w % 2 == 0 else -step)) % NZ, w))
        for x in range(NX) for z in range(NZ) for w in range(2 * NY)
    ]


def zh_perm(step):
    return [(x * NZH + z, x * NZH + (z + step) % NZH) for x in range(NX) for z in range(NZH)]


def y_perm(step):
    return [(y * 2 + c, (y + step) % NY * 2 + c) for y in range(NY) for c in range(2)]


def params():
    return pltpu.CompilerParams(vmem_limit_bytes=40 * 1024 * 1024)


def rank_blocks_kernel(lang_ref, returned_ref, out_ref):
    here = lax.axis_index("dp")
    count = jnp.int32(0)
    for owner in range(OWNERS):
        slot = jnp.int32(0)
        for k in range(PER_OWNER):
            hit = lang_ref[owner * PER_OWNER + k] == here
            slot = jnp.where(hit, count, slot)
            count = count + hit.astype(jnp.int32)
        out_ref[owner // NZH, owner % NZH * ROWS:(owner % NZH + 1) * ROWS] = returned_ref[slot]


def window_positions(z, core):
    sign = 1 - 2 * core
    return [(z + NZ + sign * step) % NZ for step in (2, 1, -1, 0)]


def window_blocks_kernel(lang_ref, in_ref, *out_refs):
    here = lax.axis_index("dp")
    column = here // NZH
    core = lax.axis_index("wout") % 2
    w = lax.axis_index("win")
    for h in range(NZH):
        for s, position in enumerate(window_positions((here + h) % NZH * NW + w, core)):
            rank = lang_ref[column * NZ + position]
            start = pl.multiple_of(position // NW * ROWS, ROWS)
            out_refs[h][s * ROWS:(s + 1) * ROWS] = in_ref[rank // NZH, pl.ds(start, ROWS)]


def window_pick_kernel(lang_ref, *refs):
    in_refs, out_ref = refs[:NZH], refs[NZH]
    here = lax.axis_index("dp")
    core = lax.axis_index("wout") % 2
    z = here % NZH * NW + lax.axis_index("win")
    for s, position in enumerate(window_positions(z, core)):
        rows = slice(s * ROWS, (s + 1) * ROWS)
        back = (here + NZH - lang_ref[here // NZH * NZ + position] % NZH) % NZH
        block = in_refs[0][rows]
        for j in range(1, NZH):
            block = jnp.where(back == j, in_refs[j][rows], block)
        out_ref[rows] = block


def product_kernel(count, *refs):
    rows_refs, (sibling_ref, own_ref), out_refs = refs[:count], refs[count:count + 2], refs[count + 2:]
    hidden, width = sibling_ref.shape
    rows = jnp.concatenate(
        [
            ref[:, s * ROWS:(s + 1) * ROWS].reshape(-1, width)
            for s in range(SLOTS) for ref in rows_refs
        ],
        axis=0,
    )

    def run(weight_ref, start):
        for tile in range(0, hidden, HIDDEN_TILE):
            value = lax.dot_general(
                rows, weight_ref[tile:tile + HIDDEN_TILE], (((1,), (1,)), ((), ())),
                preferred_element_type=jnp.float32,
            ).astype(jnp.bfloat16)
            for s, out_ref in enumerate(out_refs):
                size = out_ref.shape[0]
                out_ref[:, start + tile:start + tile + HIDDEN_TILE] = value[s * size:(s + 1) * size]

    run(sibling_ref, hidden)
    run(own_ref, 0)


def product(blocks, own, sibling):
    hidden, width = own.shape
    vmem = pl.BlockSpec(memory_space=pltpu.VMEM)
    return pl.pallas_call(
        functools.partial(product_kernel, len(blocks)),
        in_specs=[vmem] * (len(blocks) + 2),
        out_specs=[vmem] * SLOTS,
        out_shape=[jax.ShapeDtypeStruct((HALF * ROWS, 2 * hidden), jnp.bfloat16)] * SLOTS,
        compiler_params=params(),
    )(*blocks, sibling, own)


def parity_and_core():
    place = lax.axis_index("wout")
    return place // 2 % 2, place % 2


def half_sums(parts, j, i, hidden):
    total = 0.0
    for ref in parts:
        total = total + ref[j * ROWS:(j + 1) * ROWS, i * hidden:(i + 1) * hidden].astype(jnp.float32)
    return total


def send_kernel(*refs):
    parts, sent_ref = (refs[:3], refs[3:6]), refs[6]
    for h in range(2):
        for j in range(HALF):
            sent_ref[h, j] = half_sums(parts[h], j, 1, sent_ref.shape[3]).astype(jnp.bfloat16)


def keep_kernel(*refs):
    parts, (pre_ref, kept_ref, slope_ref) = (refs[:3], refs[3:6]), refs[6:]
    parity, core = parity_and_core()
    for h in range(2):
        for j in range(HALF):
            slope = gelu_slope(pre_ref[j, (parity + h) % 2, core].astype(jnp.float32))
            kept_ref[h, j] = (half_sums(parts[h], j, 0, kept_ref.shape[3]) * slope).astype(jnp.bfloat16)
            slope_ref[h, j] = gelu_slope(pre_ref[j, (parity + h) % 2, 1 - core].astype(jnp.float32))


def join_kernel(kept_ref, slope_ref, other_ref, out_ref):
    parity, core = parity_and_core()
    for h in range(2):
        for j in range(HALF):
            out_ref[j, (parity + h) % 2, core] = kept_ref[h, j]
            other = other_ref[h, j].astype(jnp.float32) * slope_ref[h, j]
            out_ref[j, (parity + h) % 2, 1 - core] = other.astype(jnp.bfloat16)


def local(returned, lang_rank, weight_down, pre_act):
    width = returned.shape[2]
    hidden = weight_down.shape[0]
    smem = pl.BlockSpec(memory_space=pltpu.SMEM)
    vmem = pl.BlockSpec(memory_space=pltpu.VMEM)

    def move(kernel, out, *values, count=None):
        shape = jax.ShapeDtypeStruct(out + (width,), jnp.bfloat16)
        return pl.pallas_call(
            kernel,
            in_specs=[smem] + [vmem] * len(values),
            out_specs=vmem if count is None else [vmem] * count,
            out_shape=shape if count is None else [shape] * count,
            compiler_params=params(),
        )(lang_rank, *values)

    sibling = lax.ppermute(weight_down, "wout", CORE_SWAP)
    held = move(rank_blocks_kernel, (NX, NZH * ROWS), returned)
    held = lax.all_to_all(held, "dp", 0, 0, axis_index_groups=X_GROUPS)
    windows = move(window_blocks_kernel, (SLOTS * ROWS,), held, count=NZH)
    windows = [windows[0]] + [lax.ppermute(windows[j], "dp", zh_perm(j)) for j in range(1, NZH)]
    window = move(window_pick_kernel, (SLOTS * ROWS,), *windows)
    near = lax.all_gather(window, "wout", axis_index_groups=PARITY_GROUPS)
    others = [
        lax.ppermute(near[:HALF // 2], "wout", y_perm(1)),
        lax.ppermute(near[HALF // 2:], "wout", y_perm(-1)),
    ]

    parts = []
    for blocks in ([near], others):
        far, ahead, behind, mine = product(blocks, weight_down, sibling)
        far = lax.ppermute(far, RING, ring_perm(1))
        behind = lax.ppermute(behind, RING, ring_perm(-1))
        ahead = (ahead.astype(jnp.float32) + far.astype(jnp.float32)).astype(jnp.bfloat16)
        parts += [mine, lax.ppermute(ahead, RING, ring_perm(1)), behind]

    def call(kernel, shapes, *values):
        return pl.pallas_call(
            kernel,
            in_specs=[vmem] * len(values),
            out_specs=[vmem] * len(shapes),
            out_shape=[jax.ShapeDtypeStruct(*shape) for shape in shapes],
            compiler_params=params(),
        )(*values)

    halves = (2, HALF, ROWS, hidden)
    split = (HALF, 2, 2, ROWS, hidden)
    (sent,) = call(send_kernel, [(halves, jnp.bfloat16)], *parts)
    other = lax.ppermute(sent, "wout", CORE_SWAP)
    kept, slope = call(
        keep_kernel,
        [(halves, jnp.bfloat16), (halves, jnp.float32)],
        *parts, pre_act.reshape(split),
    )
    (out,) = call(join_kernel, [(split, jnp.bfloat16)], kept, slope, other)
    return out.reshape(2 * NY * ROWS, hidden)


def solution(mesh):
    in_specs = (P("dp", "wout", "win"), P(), P("wout", "win"), P(("dp", "win"), "wout"))
    out_specs = P(("dp", "win"), "wout")
    return jax.shard_map(local, mesh=mesh, in_specs=in_specs, out_specs=out_specs, check_vma=False)
```
